32 devices in a mesh: groups: 2 (over x), dp: 16 (over z, y, core).
Axes of the slice: x: 2, y: 2, z: 4, core: 2. Of those that a mesh axis runs over, the one named last changes fastest.
Arguments:
- activations: bfloat16 [8192, 14336], P(('groups', 'dp')), parts along dimension 0, may hold values from -134 to 134
- out_grads: bfloat16 [8192, 4096], P(('groups', 'dp')), parts along dimension 0, may hold values from -45 to 45
- proj_in: bfloat16 [14336, 64], replicated, may hold values from -12 to 12
- proj_out: bfloat16 [4096, 64], replicated, may hold values from -12 to 12
- lengths: int32 [256], P(('groups', 'dp')), parts along dimension 0, may hold values from 1 to 32
- token_mask: int32 [8192], P(('groups', 'dp')), parts along dimension 0, may hold values 0 or 1
- query_ids: int32 [192], P(('groups', 'dp')), parts along dimension 0, may hold values from 0 to 7
- train_grads: bfloat16 [4096, 4096], P(('groups', 'dp')), parts along dimension 0, may hold values from -0.25 to 0.25
Outputs:
- influence: float32 [4096, 96], P(('groups', 'dp')), parts along dimension 0
The draws below stay inside these ranges and needn't reach their ends.
There are 2 independent parts, one for each index of `groups`. The reference program is written for one: setup_inputs(seed, part) draws one part's arguments, and reference() takes and returns one part's arrays. A program takes and returns all parts, laid end to end along the dimension named above; an argument that names none is the same for every part. Nothing has to cross between parts.
All inputs are finite; a program needn't handle non-finite values. No bound on the sum of `token_mask` on one device may be relied on, other than what follows from the above.
Results may differ from the reference program's by a relative error of at most 0.0029.
Values may be sent and summed in bfloat16 or wider, within the bound.
A program may use at most 128 MiB of HBM per device.

```python
import math
import jax
import jax.numpy as jnp
from jax import lax

D = 4096
FF = 14336
RANK = 64
LEN = 32
RESP_DEV = 8
QD = 6
TOKENS = 4096
RESPONSES = 128
QUERIES = 96
TRAIN_ROWS = 2048
N_DP = 16


def base_values(key, shape):
    values = jax.random.normal(key, shape, jnp.float32)
    return jnp.clip(values, -4.0, 4.0)


def log_scales(key, shape, low, high):
    return jnp.exp(jax.random.uniform(key, shape, jnp.float32, math.log(low), math.log(high)))


def draw_activations(key, part):
    key = jax.random.fold_in(key, 11)
    key_base, key_rows, key_cols = jax.random.split(key, 3)
    device = (jnp.arange(TOKENS) // (RESP_DEV * LEN)).astype(jnp.float32)
    ramp = 3.0 ** (device / max(N_DP - 1, 1))
    rows = log_scales(key_rows, (TOKENS, 1), 1.0, 10.0) / 3.0
    cols = log_scales(key_cols, (1, FF), 1.0, 10.0) / 3.0
    values = base_values(key_base, (TOKENS, FF)) * rows * cols * ramp[:, None]
    return values.astype(jnp.bfloat16)


def draw_out_grads(key, part):
    key = jax.random.fold_in(key, 12)
    key_base, key_rows, key_cols = jax.random.split(key, 3)
    rows = log_scales(key_rows, (TOKENS, 1), 1.0, 10.0) / 3.0
    cols = log_scales(key_cols, (1, D), 1.0, 10.0) / 3.0
    return (base_values(key_base, (TOKENS, D)) * rows * cols).astype(jnp.bfloat16)


def draw_proj_in(key, part):
    key = jax.random.fold_in(key, 13)
    key_base, key_cols = jax.random.split(key)
    cols = log_scales(key_cols, (1, RANK), 0.3, 3.0)
    return (base_values(key_base, (FF, RANK)) * cols / math.sqrt(FF)).astype(jnp.bfloat16)


def draw_proj_out(key, part):
    key = jax.random.fold_in(key, 14)
    key_base, key_cols = jax.random.split(key)
    cols = log_scales(key_cols, (1, RANK), 0.3, 3.0)
    return (base_values(key_base, (D, RANK)) * cols / math.sqrt(D)).astype(jnp.bfloat16)


def draw_train_grads(key, part):
    key = jax.random.fold_in(key, 15)
    key_base, key_rows = jax.random.split(key)
    rows = log_scales(key_rows, (TRAIN_ROWS, 1), 1.0, 10.0) / 192.0
    return (base_values(key_base, (TRAIN_ROWS, RANK * RANK)) * rows).astype(jnp.bfloat16)


def plant(drawn, stream_key, low, largest):
    index_at = [jax.random.randint(jax.random.fold_in(stream_key, axis), (), 0, length) for axis, length in enumerate(drawn.shape)]
    widest = drawn.shape.index(max(drawn.shape))
    neighbour = index_at[:widest] + [(index_at[widest] + 1) % drawn.shape[widest]] + index_at[widest + 1:]
    return drawn.at[tuple(index_at)].set(low).at[tuple(neighbour)].set(largest)


def setup_inputs(seed: int = 0, part: int = 0) -> dict:
    keys = jax.random.split(jax.random.key(seed), 9)
    part_keys = jax.random.split(jax.random.fold_in(keys[8], part), 9)
    return {
        "activations": draw_activations(jax.random.fold_in(jax.random.fold_in(keys[8], part), 71), part),
        "out_grads": draw_out_grads(jax.random.fold_in(jax.random.fold_in(keys[8], part), 71), part),
        "proj_in": draw_proj_in(jax.random.fold_in(keys[8], 71), part),
        "proj_out": draw_proj_out(jax.random.fold_in(keys[8], 71), part),
        "lengths": plant(jax.random.randint(part_keys[4], (RESPONSES,), 1, LEN + 1), jax.random.fold_in(part_keys[4], 1), 1, LEN).astype(jnp.int32),
        "token_mask": plant((jax.random.randint(part_keys[5], (TOKENS,), 0, 4) < 3).astype(jnp.int32), jax.random.fold_in(part_keys[5], 1), 0, 1),
        "query_ids": plant(jax.random.randint(part_keys[6], (QUERIES,), 0, RESP_DEV), jax.random.fold_in(part_keys[6], 1), 0, RESP_DEV - 1).astype(jnp.int32),
        "train_grads": draw_train_grads(jax.random.fold_in(jax.random.fold_in(keys[8], part), 71), part),
    }


def damp_factor(fisher):
    scale = jnp.trace(fisher) / fisher.shape[0] + 1e-06
    return jnp.linalg.cholesky(fisher / scale + 0.1 * jnp.eye(fisher.shape[0], dtype=fisher.dtype))

def reference(activations, out_grads, proj_in, proj_out, lengths, token_mask, query_ids, train_grads):
    act_proj = jnp.dot(activations.astype(jnp.float32), proj_in.astype(jnp.float32), preferred_element_type=jnp.float32)
    grad_proj = jnp.dot(out_grads.astype(jnp.float32), proj_out.astype(jnp.float32), preferred_element_type=jnp.float32)
    valid = jnp.arange(LEN)[None, :] < lengths[:, None]
    weight = (valid.reshape(-1) & (token_mask == 1)).astype(act_proj.dtype)
    grad_weighted = grad_proj * weight[:, None]
    fisher_act = jnp.dot((act_proj * weight[:, None]).T, act_proj, precision=lax.Precision.HIGHEST)
    fisher_grad = jnp.dot(grad_weighted.T, grad_proj, precision=lax.Precision.HIGHEST)
    chol_act = damp_factor(fisher_act)
    chol_grad = damp_factor(fisher_grad)
    resp_grad = jnp.einsum('rto,rti->roi', grad_weighted.reshape(RESPONSES, LEN, RANK), act_proj.reshape(RESPONSES, LEN, RANK), precision=lax.Precision.HIGHEST)
    picked = (jnp.arange(QUERIES) // QD * RESP_DEV + query_ids).astype(jnp.int32)
    chosen = resp_grad[picked]
    left = jax.vmap(lambda matrix: jax.scipy.linalg.cho_solve((chol_grad, True), matrix))(chosen)
    precond = jax.vmap(lambda matrix: jax.scipy.linalg.cho_solve((chol_act, True), matrix.T).T)(left)
    flat_rows = precond.reshape(QUERIES, RANK * RANK)
    query_rows = (flat_rows / jnp.sqrt(lax.optimization_barrier(jnp.mean(flat_rows * flat_rows, axis=1, keepdims=True)) + 1e-06)).astype(jnp.bfloat16)
    return lax.dot_general(train_grads.astype(jnp.float32), query_rows.astype(jnp.float32), (((1,), (1,)), ((), ())), preferred_element_type=jnp.float32)
```

```python
import functools

import jax
import jax.numpy as jnp
from jax import lax
from jax.experimental import pallas as pl
from jax.experimental.pallas import tpu as pltpu
from jax.sharding import PartitionSpec as P

MESH = pl.DeviceIdType.MESH
HIGHEST = lax.Precision.HIGHEST
CHUNK = 2048
PANEL = 4


def dot_t(a, b, dims, **kw):
    return lax.dot_general(a, b, (dims, ((), ())), preferred_element_type=jnp.float32, **kw)


def invert_pair(matrix):
    rank, width = matrix.shape
    tiles = [matrix[8 * t : 8 * t + 8, :] for t in range(rank // 8)]
    lane = lax.broadcasted_iota(jnp.int32, (8, width), 1)
    sub = lax.broadcasted_iota(jnp.int32, (8, width), 0)
    first = lane < rank
    column = jnp.where(first, lane, lane - rank)
    for base in range(0, rank, PANEL):
        own, start = base // 8, base % 8
        spread = [
            [
                jnp.where(
                    first,
                    jnp.broadcast_to(tile[:, base + j : base + j + 1], (8, width)),
                    jnp.broadcast_to(tile[:, rank + base + j : rank + base + j + 1], (8, width)),
                )
                for tile in tiles
            ]
            for j in range(PANEL)
        ]
        for j in range(PANEL):
            at = start + j
            here = sub == at
            at_col = column == base + j
            inv = 1.0 / spread[j][own][at : at + 1, :]
            row = jnp.where(at_col[0:1, :], 1.0, tiles[own][at : at + 1, :]) * inv
            for t in range(len(tiles)):
                new = jnp.where(at_col, 0.0, tiles[t]) - spread[j][t] * row
                tiles[t] = jnp.where(here, row, new) if t == own else new
            for k in range(j + 1, PANEL):
                factor = spread[k][own][at : at + 1, :] * inv
                for t in range(len(tiles)):
                    new = spread[k][t] - spread[j][t] * factor
                    spread[k][t] = jnp.where(here, factor, new) if t == own else new
    return jnp.concatenate(tiles, axis=0)


def kernel(
    n, lengths, query_ids, mask, act_hbm, grad_hbm, pin_hbm, pout_hbm, train_hbm, out,
    act_v, grad_v, pin_v, pout_v, train_v, part, landed, sums, total, wide, rows,
    load_sem, rs_send, rs_recv, ex_send, ex_recv, ag_send, ag_recv, row_send, row_recv,
):
    me = lax.axis_index("dp")
    tokens, n_in = act_hbm.shape
    n_out = grad_hbm.shape[1]
    rank = pin_hbm.shape[1]
    width = 2 * rank
    owners = part.shape[0]
    span_rows = part.shape[1]
    rep = n // owners

    loads = []
    sem_at = 0
    plan = []
    for x_hbm, w_hbm, x_v, w_v, depth in (
        (act_hbm, pin_hbm, act_v, pin_v, n_in),
        (grad_hbm, pout_hbm, grad_v, pout_v, n_out),
    ):
        for c in range(depth // CHUNK):
            cols = slice(c * CHUNK, (c + 1) * CHUNK)
            copies = (
                pltpu.make_async_copy(w_hbm.at[cols, :], w_v.at[cols, :], load_sem.at[sem_at]),
                pltpu.make_async_copy(x_hbm.at[:, cols], x_v.at[:, cols], load_sem.at[sem_at + 1]),
            )
            sem_at += 2
            for copy in copies:
                copy.start()
            plan.append((copies, x_v, w_v, cols))
    train_copy = pltpu.make_async_copy(train_hbm, train_v, load_sem.at[sem_at])
    train_copy.start()

    barrier = pltpu.get_barrier_semaphore()

    def greet(k, _):
        pl.semaphore_signal(
            barrier, inc=1, device_id={"dp": lax.rem(me + k, n)}, device_id_type=MESH
        )
        return 0

    lax.fori_loop(1, n, greet, 0)

    accs = {}
    for copies, x_v, w_v, cols in plan:
        for copy in copies:
            copy.wait()
        term = jnp.dot(x_v[:, cols], w_v[cols, :], preferred_element_type=jnp.float32)
        accs[id(x_v)] = accs[id(x_v)] + term if id(x_v) in accs else term
    act_proj, grad_proj = accs[id(act_v)], accs[id(grad_v)]

    slot = lax.broadcasted_iota(jnp.int32, (1, tokens), 1)
    n_resp = lengths.shape[0]
    span = tokens // n_resp
    response = slot // span
    length = jnp.zeros((1, tokens), jnp.int32)
    for r in range(n_resp):
        length = jnp.where(response == r, lengths[r], length)
    weight = jnp.where((slot - response * span < length) & (mask[...] == 1), 1.0, 0.0)

    both = jnp.concatenate([act_proj, grad_proj], axis=1)
    both_t = both.T * weight
    fisher = jnp.dot(both_t, both, precision=HIGHEST, preferred_element_type=jnp.float32)
    lane = lax.broadcasted_iota(jnp.int32, (rank, width), 1)
    packed = jnp.where(lane < rank, fisher[:rank, :], fisher[rank:, :])
    for c in range(owners):
        part[c] = packed[c * span_rows : (c + 1) * span_rows, :]

    pl.semaphore_wait(barrier, n - 1)

    team = me // owners
    seat = me - team * owners

    def peer(k):
        return lax.rem(seat + k, owners)

    def rs_copy(k):
        to = peer(k)
        return pltpu.make_async_remote_copy(
            src_ref=part.at[to], dst_ref=landed.at[k],
            send_sem=rs_send.at[k], recv_sem=rs_recv.at[k],
            device_id={"dp": team * owners + to}, device_id_type=MESH,
        )

    def start_rs(k, _):
        rs_copy(k).start()
        return 0

    lax.fori_loop(1, owners, start_rs, 0)

    n_query = query_ids.shape[0]
    grad_t = both_t[rank:, :]
    picked = jnp.concatenate(
        [jnp.where(response == query_ids[q], grad_t, 0.0) for q in range(n_query)], axis=0
    )
    chosen = jnp.dot(picked, act_proj, precision=HIGHEST, preferred_element_type=jnp.float32)

    def wait_rs(k, acc):
        rs_copy(k).wait()
        return acc + landed[k]

    mine = lax.fori_loop(1, owners, wait_rs, part[seat])
    if rep > 1:
        sums[0] = mine

        def ex_copy(k):
            return pltpu.make_async_remote_copy(
                src_ref=sums.at[0], dst_ref=sums.at[k],
                send_sem=ex_send.at[k], recv_sem=ex_recv.at[k],
                device_id={"dp": lax.rem(me + k * owners, n)}, device_id_type=MESH,
            )

        def start_ex(k, _):
            ex_copy(k).start()
            return 0

        def wait_ex(k, acc):
            ex_copy(k).wait()
            return acc + sums[k]

        lax.fori_loop(1, rep, start_ex, 0)
        mine = lax.fori_loop(1, rep, wait_ex, mine)
    total[seat] = mine

    def ag_copy(k):
        return pltpu.make_async_remote_copy(
            src_ref=total.at[seat], dst_ref=total.at[seat],
            send_sem=ag_send.at[k], recv_sem=ag_recv.at[k],
            device_id={"dp": team * owners + peer(k)}, device_id_type=MESH,
        )

    def start_ag(k, _):
        ag_copy(k).start()
        return 0

    def wait_ag(k, _):
        ag_copy(k).wait()
        return 0

    lax.fori_loop(1, owners, start_ag, 0)
    lax.fori_loop(1, owners, wait_ag, 0)

    summed = jnp.concatenate([total[c] for c in range(owners)], axis=0)
    row_at = lax.broadcasted_iota(jnp.int32, (rank, width), 0)
    left = lane < rank
    diag = row_at == jnp.where(left, lane, lane - rank)
    on_diag = jnp.where(diag, summed, 0.0)
    trace_act = jnp.sum(jnp.where(left, on_diag, 0.0), axis=(0, 1), keepdims=True)
    trace_grad = jnp.sum(jnp.where(left, 0.0, on_diag), axis=(0, 1), keepdims=True)
    scale = jnp.where(left, trace_act, trace_grad) / rank + 1e-06
    inverse = invert_pair(summed / scale + jnp.where(diag, 0.1, 0.0))

    swapped = pltpu.roll(inverse, rank, 1)
    inv_act_twice = jnp.where(left, inverse, swapped)
    inv_grad = swapped[:, :rank]
    right_done = jnp.dot(chosen, inv_act_twice, precision=HIGHEST, preferred_element_type=jnp.float32)
    for q in range(8):
        if q < n_query:
            value = jnp.dot(
                inv_grad, right_done[q * rank : (q + 1) * rank, :],
                precision=HIGHEST, preferred_element_type=jnp.float32,
            )
        else:
            value = jnp.zeros((rank, width), jnp.float32)
        wide[pl.ds(q, rank, stride=8), :] = value
    left8 = left[:8, :]
    pieces = [
        jnp.where(left8, wide[16 * p : 16 * p + 8, :], wide[16 * p + 8 : 16 * p + 16, :])
        for p in range(rank // 2)
    ]
    squares = pieces[0] * pieces[0]
    for piece in pieces[1:]:
        squares = squares + piece * piece
    mean = jnp.sum(squares, axis=1, keepdims=True) / (rank * rank)
    root = jnp.sqrt(mean + 1e-06)
    half = rank // 4
    for p in range(half):
        tile = jnp.concatenate([pieces[p] / root, pieces[p + half] / root], axis=0)
        rows[me, :, width * p : width * (p + 1)] = tile.astype(jnp.bfloat16)

    fours = n // 4
    place = lax.rem(me, 4)
    far = me + 2 - 4 * (place // 2)
    near = me + 1 - 2 * lax.rem(me, 2)

    def line(k):
        return lax.rem(me + 4 * k, n)

    def back(k):
        return lax.rem(me + n - 4 * k, n)

    def send(block, to, k):
        return pltpu.make_async_remote_copy(
            src_ref=rows.at[block], dst_ref=rows.at[block],
            send_sem=row_send.at[k], recv_sem=row_recv.at[k],
            device_id={"dp": to}, device_id_type=MESH,
        )

    def along(k):
        return send(me, line(k), k)

    def to_far(k):
        return send(back(k), far, fours + k)

    def to_near(k):
        return send(back(k), near, 2 * fours + k)

    def to_near_far(k):
        return send(lax.rem(far + n - 4 * k, n), near, 3 * fours + k)

    def start_line(k, _):
        along(k).start()
        return 0

    def forward(k, _):
        @pl.when(k > 0)
        def _():
            along(k).wait_recv()

        to_far(k).start()
        to_near(k).start()
        return 0

    def forward_far(k, _):
        to_far(k).wait_recv()
        to_near_far(k).start()
        return 0

    def finish(k, _):
        @pl.when(k > 0)
        def _():
            along(k).wait_send()

        to_far(k).wait_send()
        to_near(k).wait()
        to_near_far(k).wait()
        return 0

    lax.fori_loop(1, fours, start_line, 0)
    lax.fori_loop(0, fours, forward, 0)
    lax.fori_loop(0, fours, forward_far, 0)
    lax.fori_loop(0, fours, finish, 0)

    train_copy.wait()
    cut = rows.shape[2]
    gathered = rows[...].reshape(n * 16, cut)
    low = dot_t(train_v[:, :cut], gathered, ((1,), (1,)))
    high = dot_t(train_v[:, cut:], gathered, ((1,), (1,)))
    at = lax.broadcasted_iota(jnp.int32, (n * 16, n * n_query), 0)
    want = lax.broadcasted_iota(jnp.int32, (n * 16, n * n_query), 1)
    want = want // n_query * 16 + lax.rem(want, n_query)
    out[...] = jnp.dot(
        low, jnp.where(at == want, 1.0, 0.0), precision=HIGHEST, preferred_element_type=jnp.float32
    ) + jnp.dot(
        high, jnp.where(at == want + 8, 1.0, 0.0), precision=HIGHEST, preferred_element_type=jnp.float32
    )


def body(n, activations, out_grads, proj_in, proj_out, lengths, token_mask, query_ids, train_grads):
    tokens, n_in = activations.shape
    n_out = out_grads.shape[1]
    rank = proj_in.shape[1]
    n_query = query_ids.shape[0]
    owners = min(n, 16)
    span_rows = rank // owners
    n_loads = 2 * (n_in // CHUNK + n_out // CHUNK) + 1
    smem = pl.BlockSpec(memory_space=pltpu.SMEM)
    vmem = pl.BlockSpec(memory_space=pltpu.VMEM)
    hbm = pl.BlockSpec(memory_space=pl.ANY)
    dma = pltpu.SemaphoreType.DMA
    flops = 2 * tokens * rank * (n_in + n_out) + 2 * train_grads.size * n * n_query
    return pl.pallas_call(
        functools.partial(kernel, n),
        out_shape=jax.ShapeDtypeStruct((train_grads.shape[0], n * n_query), jnp.float32),
        in_specs=[smem, smem, vmem, hbm, hbm, hbm, hbm, hbm],
        out_specs=vmem,
        scratch_shapes=[
            pltpu.VMEM(activations.shape, jnp.bfloat16),
            pltpu.VMEM(out_grads.shape, jnp.bfloat16),
            pltpu.VMEM(proj_in.shape, jnp.bfloat16),
            pltpu.VMEM(proj_out.shape, jnp.bfloat16),
            pltpu.VMEM(train_grads.shape, jnp.bfloat16),
            pltpu.VMEM((owners, span_rows, 2 * rank), jnp.float32),
            pltpu.VMEM((owners, span_rows, 2 * rank), jnp.float32),
            pltpu.VMEM((max(n // owners, 1), span_rows, 2 * rank), jnp.float32),
            pltpu.VMEM((owners, span_rows, 2 * rank), jnp.float32),
            pltpu.VMEM((rank * 8, 2 * rank), jnp.float32),
            pltpu.VMEM((n, 16, rank * rank // 2), jnp.bfloat16),
            dma((n_loads,)),
            dma((owners,)),
            dma((owners,)),
            dma((max(n // owners, 1),)),
            dma((max(n // owners, 1),)),
            dma((owners,)),
            dma((owners,)),
            dma((n,)),
            dma((n,)),
        ],
        compiler_params=pltpu.CompilerParams(
            collective_id=0, has_side_effects=True, vmem_limit_bytes=56 * 1024 * 1024
        ),
        cost_estimate=pl.CostEstimate(flops=flops, bytes_accessed=16_000_000, transcendentals=0),
    )(
        lengths, query_ids, token_mask.reshape(1, tokens),
        activations, out_grads, proj_in, proj_out, train_grads,
    )


def solution(mesh):
    in_specs = (
        P(("groups", "dp"), None),
        P(("groups", "dp"), None),
        P(),
        P(),
        P(("groups", "dp")),
        P(("groups", "dp")),
        P(("groups", "dp")),
        P(("groups", "dp"), None),
    )
    out_specs = P(("groups", "dp"), None)
    run = functools.partial(body, mesh.shape["dp"])
    return jax.shard_map(run, mesh=mesh, in_specs=in_specs, out_specs=out_specs, check_vma=False)
```

```python
import functools

import jax
import jax.numpy as jnp
from jax import lax
from jax.experimental import pallas as pl
from jax.experimental.pallas import tpu as pltpu
from jax.sharding import PartitionSpec as P

MESH = pl.DeviceIdType.MESH
HIGHEST = lax.Precision.HIGHEST
CHUNK = 2048
PANEL = 4


def dot_t(a, b, dims, **kw):
    return lax.dot_general(a, b, (dims, ((), ())), preferred_element_type=jnp.float32, **kw)


def invert_pair(matrix):
    rank, width = matrix.shape
    tiles = [matrix[8 * t : 8 * t + 8, :] for t in range(rank // 8)]
    lane = lax.broadcasted_iota(jnp.int32, (8, width), 1)
    sub = lax.broadcasted_iota(jnp.int32, (8, width), 0)
    first = lane < rank
    column = jnp.where(first, lane, lane - rank)
    for base in range(0, rank, PANEL):
        own, start = base // 8, base % 8
        spread = [
            [
                jnp.where(
                    first,
                    jnp.broadcast_to(tile[:, base + j : base + j + 1], (8, width)),
                    jnp.broadcast_to(tile[:, rank + base + j : rank + base + j + 1], (8, width)),
                )
                for tile in tiles
            ]
            for j in range(PANEL)
        ]
        for j in range(PANEL):
            at = start + j
            here = sub == at
            at_col = column == base + j
            inv = 1.0 / spread[j][own][at : at + 1, :]
            row = jnp.where(at_col[0:1, :], 1.0, tiles[own][at : at + 1, :]) * inv
            for t in range(len(tiles)):
                new = jnp.where(at_col, 0.0, tiles[t]) - spread[j][t] * row
                tiles[t] = jnp.where(here, row, new) if t == own else new
            for k in range(j + 1, PANEL):
                factor = spread[k][own][at : at + 1, :] * inv
                for t in range(len(tiles)):
                    new = spread[k][t] - spread[j][t] * factor
                    spread[k][t] = jnp.where(here, factor, new) if t == own else new
    return jnp.concatenate(tiles, axis=0)


def kernel(
    n, lengths, query_ids, mask, act_hbm, grad_hbm, pin_hbm, pout_hbm, train_hbm, out,
    act_v, grad_v, pin_v, pout_v, train_v, part, landed, sums, total, wide, rows,
    load_sem, rs_send, rs_recv, ex_send, ex_recv, ag_send, ag_recv, row_send, row_recv,
):
    me = lax.axis_index("dp")
    tokens, n_in = act_hbm.shape
    n_out = grad_hbm.shape[1]
    rank = pin_hbm.shape[0]
    width = 2 * rank
    owners = part.shape[0]
    span_rows = part.shape[1]
    rep = n // owners

    loads = []
    sem_at = 0
    plan = []
    for x_hbm, w_hbm, x_v, w_v, depth in (
        (act_hbm, pin_hbm, act_v, pin_v, n_in),
        (grad_hbm, pout_hbm, grad_v, pout_v, n_out),
    ):
        for c in range(depth // CHUNK):
            cols = slice(c * CHUNK, (c + 1) * CHUNK)
            copies = (
                pltpu.make_async_copy(w_hbm.at[:, cols], w_v.at[:, cols], load_sem.at[sem_at]),
                pltpu.make_async_copy(x_hbm.at[:, cols], x_v.at[:, cols], load_sem.at[sem_at + 1]),
            )
            sem_at += 2
            for copy in copies:
                copy.start()
            plan.append((copies, x_v, w_v, cols))
    train_copy = pltpu.make_async_copy(train_hbm, train_v, load_sem.at[sem_at])
    train_copy.start()

    barrier = pltpu.get_barrier_semaphore()

    def greet(k, _):
        pl.semaphore_signal(
            barrier, inc=1, device_id={"dp": lax.rem(me + k, n)}, device_id_type=MESH
        )
        return 0

    lax.fori_loop(1, n, greet, 0)

    accs = {}
    for copies, x_v, w_v, cols in plan:
        for copy in copies:
            copy.wait()
        term = dot_t(x_v[:, cols], w_v[:, cols], ((1,), (1,)))
        accs[id(x_v)] = accs[id(x_v)] + term if id(x_v) in accs else term
    act_proj, grad_proj = accs[id(act_v)], accs[id(grad_v)]

    slot = lax.broadcasted_iota(jnp.int32, (1, tokens), 1)
    n_resp = lengths.shape[0]
    span = tokens // n_resp
    response = slot // span
    length = jnp.zeros((1, tokens), jnp.int32)
    for r in range(n_resp):
        length = jnp.where(response == r, lengths[r], length)
    weight = jnp.where((slot - response * span < length) & (mask[...] == 1), 1.0, 0.0)

    both = jnp.concatenate([act_proj, grad_proj], axis=1)
    both_t = both.T * weight
    fisher = jnp.dot(both_t, both, precision=HIGHEST, preferred_element_type=jnp.float32)
    lane = lax.broadcasted_iota(jnp.int32, (rank, width), 1)
    packed = jnp.where(lane < rank, fisher[:rank, :], fisher[rank:, :])
    for c in range(owners):
        part[c] = packed[c * span_rows : (c + 1) * span_rows, :]

    pl.semaphore_wait(barrier, n - 1)

    team = me // owners
    seat = me - team * owners

    def peer(k):
        return lax.rem(seat + k, owners)

    def rs_copy(k):
        to = peer(k)
        return pltpu.make_async_remote_copy(
            src_ref=part.at[to], dst_ref=landed.at[k],
            send_sem=rs_send.at[k], recv_sem=rs_recv.at[k],
            device_id={"dp": team * owners + to}, device_id_type=MESH,
        )

    def start_rs(k, _):
        rs_copy(k).start()
        return 0

    lax.fori_loop(1, owners, start_rs, 0)

    n_query = query_ids.shape[0]
    grad_t = both_t[rank:, :]
    picked = jnp.concatenate(
        [jnp.where(response == query_ids[q], grad_t, 0.0) for q in range(n_query)], axis=0
    )
    chosen = jnp.dot(picked, act_proj, precision=HIGHEST, preferred_element_type=jnp.float32)

    def wait_rs(k, acc):
        rs_copy(k).wait()
        return acc + landed[k]

    mine = lax.fori_loop(1, owners, wait_rs, part[seat])
    if rep > 1:
        sums[0] = mine

        def ex_copy(k):
            return pltpu.make_async_remote_copy(
                src_ref=sums.at[0], dst_ref=sums.at[k],
                send_sem=ex_send.at[k], recv_sem=ex_recv.at[k],
                device_id={"dp": lax.rem(me + k * owners, n)}, device_id_type=MESH,
            )

        def start_ex(k, _):
            ex_copy(k).start()
            return 0

        def wait_ex(k, acc):
            ex_copy(k).wait()
            return acc + sums[k]

        lax.fori_loop(1, rep, start_ex, 0)
        mine = lax.fori_loop(1, rep, wait_ex, mine)
    total[seat] = mine

    def ag_copy(k):
        return pltpu.make_async_remote_copy(
            src_ref=total.at[seat], dst_ref=total.at[seat],
            send_sem=ag_send.at[k], recv_sem=ag_recv.at[k],
            device_id={"dp": team * owners + peer(k)}, device_id_type=MESH,
        )

    def start_ag(k, _):
        ag_copy(k).start()
        return 0

    def wait_ag(k, _):
        ag_copy(k).wait()
        return 0

    lax.fori_loop(1, owners, start_ag, 0)
    lax.fori_loop(1, owners, wait_ag, 0)

    summed = jnp.concatenate([total[c] for c in range(owners)], axis=0)
    row_at = lax.broadcasted_iota(jnp.int32, (rank, width), 0)
    left = lane < rank
    diag = row_at == jnp.where(left, lane, lane - rank)
    on_diag = jnp.where(diag, summed, 0.0)
    trace_act = jnp.sum(jnp.where(left, on_diag, 0.0), axis=(0, 1), keepdims=True)
    trace_grad = jnp.sum(jnp.where(left, 0.0, on_diag), axis=(0, 1), keepdims=True)
    scale = jnp.where(left, trace_act, trace_grad) / rank + 1e-06
    inverse = invert_pair(summed / scale + jnp.where(diag, 0.1, 0.0))

    swapped = pltpu.roll(inverse, rank, 1)
    inv_act_twice = jnp.where(left, inverse, swapped)
    inv_grad = swapped[:, :rank]
    right_done = jnp.dot(chosen, inv_act_twice, precision=HIGHEST, preferred_element_type=jnp.float32)
    for q in range(8):
        if q < n_query:
            value = jnp.dot(
                inv_grad, right_done[q * rank : (q + 1) * rank, :],
                precision=HIGHEST, preferred_element_type=jnp.float32,
            )
        else:
            value = jnp.zeros((rank, width), jnp.float32)
        wide[pl.ds(q, rank, stride=8), :] = value
    left8 = left[:8, :]
    pieces = [
        jnp.where(left8, wide[16 * p : 16 * p + 8, :], wide[16 * p + 8 : 16 * p + 16, :])
        for p in range(rank // 2)
    ]
    squares = pieces[0] * pieces[0]
    for piece in pieces[1:]:
        squares = squares + piece * piece
    mean = jnp.sum(squares, axis=1, keepdims=True) / (rank * rank)
    root = jnp.sqrt(mean + 1e-06)
    half = rank // 4
    for p in range(half):
        tile = jnp.concatenate([pieces[p] / root, pieces[p + half] / root], axis=0)
        rows[me, :, width * p : width * (p + 1)] = tile.astype(jnp.bfloat16)

    fours = n // 4
    place = lax.rem(me, 4)
    far = me + 2 - 4 * (place // 2)
    near = me + 1 - 2 * lax.rem(me, 2)

    def line(k):
        return lax.rem(me + 4 * k, n)

    def back(k):
        return lax.rem(me + n - 4 * k, n)

    def send(block, to, k):
        return pltpu.make_async_remote_copy(
            src_ref=rows.at[block], dst_ref=rows.at[block],
            send_sem=row_send.at[k], recv_sem=row_recv.at[k],
            device_id={"dp": to}, device_id_type=MESH,
        )

    def along(k):
        return send(me, line(k), k)

    def to_far(k):
        return send(back(k), far, fours + k)

    def to_near(k):
        return send(back(k), near, 2 * fours + k)

    def to_near_far(k):
        return send(lax.rem(far + n - 4 * k, n), near, 3 * fours + k)

    def start_line(k, _):
        along(k).start()
        return 0

    def forward(k, _):
        @pl.when(k > 0)
        def _():
            along(k).wait_recv()

        to_far(k).start()
        to_near(k).start()
        return 0

    def forward_far(k, _):
        to_far(k).wait_recv()
        to_near_far(k).start()
        return 0

    def finish(k, _):
        @pl.when(k > 0)
        def _():
            along(k).wait_send()

        to_far(k).wait_send()
        to_near(k).wait()
        to_near_far(k).wait()
        return 0

    lax.fori_loop(1, fours, start_line, 0)
    lax.fori_loop(0, fours, forward, 0)
    lax.fori_loop(0, fours, forward_far, 0)
    lax.fori_loop(0, fours, finish, 0)

    train_copy.wait()
    cut = rows.shape[2]
    gathered = rows[...].reshape(n * 16, cut)
    low = dot_t(gathered, train_v[:, :cut], ((1,), (1,)))
    high = dot_t(gathered, train_v[:, cut:], ((1,), (1,)))
    for d in range(n):
        out[d * n_query : (d + 1) * n_query, :] = (
            low[16 * d : 16 * d + n_query, :] + high[16 * d + 8 : 16 * d + 8 + n_query, :]
        )


def body(n, activations, out_grads, proj_in, proj_out, lengths, token_mask, query_ids, train_grads):
    tokens, n_in = activations.shape
    n_out = out_grads.shape[1]
    rank = proj_in.shape[1]
    n_query = query_ids.shape[0]
    owners = min(n, 16)
    span_rows = rank // owners
    n_loads = 2 * (n_in // CHUNK + n_out // CHUNK) + 1
    smem = pl.BlockSpec(memory_space=pltpu.SMEM)
    vmem = pl.BlockSpec(memory_space=pltpu.VMEM)
    hbm = pl.BlockSpec(memory_space=pl.ANY)
    dma = pltpu.SemaphoreType.DMA
    flops = 2 * tokens * rank * (n_in + n_out) + 2 * train_grads.size * n * n_query
    return pl.pallas_call(
        functools.partial(kernel, n),
        out_shape=jax.ShapeDtypeStruct((n * n_query, train_grads.shape[0]), jnp.float32),
        in_specs=[smem, smem, vmem, hbm, hbm, hbm, hbm, hbm],
        out_specs=vmem,
        scratch_shapes=[
            pltpu.VMEM(activations.shape, jnp.bfloat16),
            pltpu.VMEM(out_grads.shape, jnp.bfloat16),
            pltpu.VMEM((rank, n_in), jnp.bfloat16),
            pltpu.VMEM((rank, n_out), jnp.bfloat16),
            pltpu.VMEM(train_grads.shape, jnp.bfloat16),
            pltpu.VMEM((owners, span_rows, 2 * rank), jnp.float32),
            pltpu.VMEM((owners, span_rows, 2 * rank), jnp.float32),
            pltpu.VMEM((max(n // owners, 1), span_rows, 2 * rank), jnp.float32),
            pltpu.VMEM((owners, span_rows, 2 * rank), jnp.float32),
            pltpu.VMEM((rank * 8, 2 * rank), jnp.float32),
            pltpu.VMEM((n, 16, rank * rank // 2), jnp.bfloat16),
            dma((n_loads,)),
            dma((owners,)),
            dma((owners,)),
            dma((max(n // owners, 1),)),
            dma((max(n // owners, 1),)),
            dma((owners,)),
            dma((owners,)),
            dma((n,)),
            dma((n,)),
        ],
        compiler_params=pltpu.CompilerParams(
            collective_id=0, has_side_effects=True, vmem_limit_bytes=56 * 1024 * 1024
        ),
        cost_estimate=pl.CostEstimate(flops=flops, bytes_accessed=16_000_000, transcendentals=0),
    )(
        lengths, query_ids, token_mask.reshape(1, tokens),
        activations, out_grads, proj_in.T, proj_out.T, train_grads,
    ).T


def solution(mesh):
    in_specs = (
        P(("groups", "dp"), None),
        P(("groups", "dp"), None),
        P(),
        P(),
        P(("groups", "dp")),
        P(("groups", "dp")),
        P(("groups", "dp")),
        P(("groups", "dp"), None),
    )
    out_specs = P(("groups", "dp"), None)
    run = functools.partial(body, mesh.shape["dp"])
    return jax.shard_map(run, mesh=mesh, in_specs=in_specs, out_specs=out_specs, check_vma=False)
```

```python
import functools

import jax
import jax.numpy as jnp
from jax import lax
from jax.experimental import pallas as pl
from jax.experimental.pallas import tpu as pltpu
from jax.sharding import PartitionSpec as P

MESH = pl.DeviceIdType.MESH
HIGHEST = lax.Precision.HIGHEST
CHUNK = 2048
PANEL = 4


def dot_t(a, b, dims, **kw):
    return lax.dot_general(a, b, (dims, ((), ())), preferred_element_type=jnp.float32, **kw)


def invert_pair(matrix):
    rank, width = matrix.shape
    tiles = [matrix[8 * t : 8 * t + 8, :] for t in range(rank // 8)]
    lane = lax.broadcasted_iota(jnp.int32, (8, width), 1)
    sub = lax.broadcasted_iota(jnp.int32, (8, width), 0)
    first = lane < rank
    column = jnp.where(first, lane, lane - rank)
    for base in range(0, rank, PANEL):
        own, start = base // 8, base % 8
        spread = [
            [
                jnp.where(
                    first,
                    jnp.broadcast_to(tile[:, base + j : base + j + 1], (8, width)),
                    jnp.broadcast_to(tile[:, rank + base + j : rank + base + j + 1], (8, width)),
                )
                for tile in tiles
            ]
            for j in range(PANEL)
        ]
        for j in range(PANEL):
            at = start + j
            here = sub == at
            at_col = column == base + j
            inv = 1.0 / spread[j][own][at : at + 1, :]
            row = jnp.where(at_col[0:1, :], 1.0, tiles[own][at : at + 1, :]) * inv
            for t in range(len(tiles)):
                new = jnp.where(at_col, 0.0, tiles[t]) - spread[j][t] * row
                tiles[t] = jnp.where(here, row, new) if t == own else new
            for k in range(j + 1, PANEL):
                factor = spread[k][own][at : at + 1, :] * inv
                for t in range(len(tiles)):
                    new = spread[k][t] - spread[j][t] * factor
                    spread[k][t] = jnp.where(here, factor, new) if t == own else new
    return jnp.concatenate(tiles, axis=0)


def kernel(
    n, lengths, query_ids, mask, act_hbm, grad_hbm, pin_hbm, pout_hbm, train_hbm, out,
    act_v, grad_v, pin_v, pout_v, train_v, part, landed, sums, total, wide, rows,
    load_sem, rs_send, rs_recv, ex_send, ex_recv, ag_send, ag_recv, row_send, row_recv,
):
    me = lax.axis_index("dp")
    tokens, n_in = act_hbm.shape
    n_out = grad_hbm.shape[1]
    rank = pin_hbm.shape[0]
    width = 2 * rank
    owners = part.shape[0]
    span_rows = part.shape[1]
    rep = n // owners

    sem_at = 0
    plan = []
    for x_hbm, w_hbm, x_v, w_v, depth in (
        (act_hbm, pin_hbm, act_v, pin_v, n_in),
        (grad_hbm, pout_hbm, grad_v, pout_v, n_out),
    ):
        for c in range(depth // CHUNK):
            cols = slice(c * CHUNK, (c + 1) * CHUNK)
            copies = (
                pltpu.make_async_copy(w_hbm.at[:, cols], w_v.at[:, cols], load_sem.at[sem_at]),
                pltpu.make_async_copy(x_hbm.at[:, cols], x_v.at[:, cols], load_sem.at[sem_at + 1]),
            )
            sem_at += 2
            for copy in copies:
                copy.start()
            plan.append((copies, x_v, w_v, cols))
    train_copy = pltpu.make_async_copy(train_hbm, train_v, load_sem.at[sem_at])
    train_copy.start()

    barrier = pltpu.get_barrier_semaphore()

    chips = n // 2
    core = lax.rem(me, 2)
    near = me + 1 - 2 * core

    def greet(to):
        pl.semaphore_signal(barrier, inc=1, device_id={"dp": to}, device_id_type=MESH)

    def greet_chip(k, _):
        greet(lax.rem(me + 2 * k, n))
        return 0

    greet(near)
    lax.fori_loop(1, chips, greet_chip, 0)

    accs = {}
    for copies, x_v, w_v, cols in plan:
        for copy in copies:
            copy.wait()
        term = dot_t(x_v[:, cols], w_v[:, cols], ((1,), (1,)))
        accs[id(x_v)] = accs[id(x_v)] + term if id(x_v) in accs else term
    act_proj, grad_proj = accs[id(act_v)], accs[id(grad_v)]

    slot = lax.broadcasted_iota(jnp.int32, (1, tokens), 1)
    n_resp = lengths.shape[0]
    span = tokens // n_resp
    response = slot // span
    length = jnp.zeros((1, tokens), jnp.int32)
    for r in range(n_resp):
        length = jnp.where(response == r, lengths[r], length)
    weight = jnp.where((slot - response * span < length) & (mask[...] == 1), 1.0, 0.0)

    both = jnp.concatenate([act_proj, grad_proj], axis=1)
    both_t = both.T * weight
    fisher = jnp.dot(both_t, both, precision=HIGHEST, preferred_element_type=jnp.float32)
    lane = lax.broadcasted_iota(jnp.int32, (rank, width), 1)
    packed = jnp.where(lane < rank, fisher[:rank, :], fisher[rank:, :])
    for c in range(owners):
        part[c] = packed[c * span_rows : (c + 1) * span_rows, :]

    pl.semaphore_wait(barrier, chips)

    team = me // owners
    seat = me - team * owners

    def peer(k):
        return lax.rem(seat + k, owners)

    def rs_copy(k):
        to = peer(k)
        return pltpu.make_async_remote_copy(
            src_ref=part.at[to], dst_ref=landed.at[k],
            send_sem=rs_send.at[k], recv_sem=rs_recv.at[k],
            device_id={"dp": team * owners + to}, device_id_type=MESH,
        )

    def start_rs(k, _):
        rs_copy(k).start()
        return 0

    lax.fori_loop(1, owners, start_rs, 0)

    n_query = query_ids.shape[0]
    grad_t = both_t[rank:, :]
    picked = jnp.concatenate(
        [jnp.where(response == query_ids[q], grad_t, 0.0) for q in range(n_query)], axis=0
    )
    chosen = jnp.dot(picked, act_proj, precision=HIGHEST, preferred_element_type=jnp.float32)

    def wait_rs(k, acc):
        rs_copy(k).wait()
        return acc + landed[k]

    mine = lax.fori_loop(1, owners, wait_rs, part[seat])
    if rep > 1:
        sums[0] = mine

        def ex_copy(k):
            return pltpu.make_async_remote_copy(
                src_ref=sums.at[0], dst_ref=sums.at[k],
                send_sem=ex_send.at[k], recv_sem=ex_recv.at[k],
                device_id={"dp": lax.rem(me + k * owners, n)}, device_id_type=MESH,
            )

        def start_ex(k, _):
            ex_copy(k).start()
            return 0

        def wait_ex(k, acc):
            ex_copy(k).wait()
            return acc + sums[k]

        lax.fori_loop(1, rep, start_ex, 0)
        mine = lax.fori_loop(1, rep, wait_ex, mine)
    total[seat] = mine

    def ag_copy(k):
        return pltpu.make_async_remote_copy(
            src_ref=total.at[seat], dst_ref=total.at[seat],
            send_sem=ag_send.at[k], recv_sem=ag_recv.at[k],
            device_id={"dp": team * owners + peer(k)}, device_id_type=MESH,
        )

    def start_ag(k, _):
        ag_copy(k).start()
        return 0

    def wait_ag(k, _):
        ag_copy(k).wait()
        return 0

    lax.fori_loop(1, owners, start_ag, 0)
    lax.fori_loop(1, owners, wait_ag, 0)

    summed = jnp.concatenate([total[c] for c in range(owners)], axis=0)
    row_at = lax.broadcasted_iota(jnp.int32, (rank, width), 0)
    left = lane < rank
    diag = row_at == jnp.where(left, lane, lane - rank)
    on_diag = jnp.where(diag, summed, 0.0)
    trace_act = jnp.sum(jnp.where(left, on_diag, 0.0), axis=(0, 1), keepdims=True)
    trace_grad = jnp.sum(jnp.where(left, 0.0, on_diag), axis=(0, 1), keepdims=True)
    scale = jnp.where(left, trace_act, trace_grad) / rank + 1e-06
    inverse = invert_pair(summed / scale + jnp.where(diag, 0.1, 0.0))

    swapped = pltpu.roll(inverse, rank, 1)
    inv_act_twice = jnp.where(left, inverse, swapped)
    inv_grad = swapped[:, :rank]
    right_done = jnp.dot(chosen, inv_act_twice, precision=HIGHEST, preferred_element_type=jnp.float32)
    for q in range(8):
        if q < n_query:
            value = jnp.dot(
                inv_grad, right_done[q * rank : (q + 1) * rank, :],
                precision=HIGHEST, preferred_element_type=jnp.float32,
            )
        else:
            value = jnp.zeros((rank, width), jnp.float32)
        wide[pl.ds(q, rank, stride=8), :] = value
    left8 = left[:8, :]
    pieces = [
        jnp.where(left8, wide[16 * p : 16 * p + 8, :], wide[16 * p + 8 : 16 * p + 16, :])
        for p in range(rank // 2)
    ]
    squares = pieces[0] * pieces[0]
    for piece in pieces[1:]:
        squares = squares + piece * piece
    mean = jnp.sum(squares, axis=1, keepdims=True) / (rank * rank)
    root = jnp.sqrt(mean + 1e-06)
    pieces = [piece / root for piece in pieces]
    sub8 = row_at[:8, :]
    body_count = rank // 2 * n_query // 8
    tail_count = rank // 2 - body_count
    third = n_query // 2
    packed_rows = []
    for p in range(body_count):
        tail, q = pieces[body_count + p % tail_count], p // tail_count
        last = jnp.where(sub8 == 6, tail[q : q + 1, :], tail[third + q : third + q + 1, :])
        packed_rows.append(jnp.where(sub8 < 6, pieces[p], last))
    half = body_count // 2
    mine_at = core * chips + me // 2
    for p in range(half):
        tile = jnp.concatenate([packed_rows[p], packed_rows[p + half]], axis=0)
        rows[mine_at, :, width * p : width * (p + 1)] = tile.astype(jnp.bfloat16)

    def send(block, to, k):
        return pltpu.make_async_remote_copy(
            src_ref=rows.at[block], dst_ref=rows.at[block],
            send_sem=row_send.at[k], recv_sem=row_recv.at[k],
            device_id={"dp": to}, device_id_type=MESH,
        )

    def to_chip(k):
        return send(mine_at, lax.rem(me + 2 * k, n), k)

    def to_near(k):
        return send(core * chips + lax.rem(me // 2 + chips - k, chips), near, chips + k)

    def start_chip(k, _):
        to_chip(k).start()
        return 0

    def hand_on(k, _):
        to_chip(k).wait_recv()
        to_near(k).start()
        return 0

    def finish(k, _):
        to_near(k).wait()
        to_chip(k).wait_send()
        return 0

    lax.fori_loop(1, chips, start_chip, 0)
    to_near(0).start()
    lax.fori_loop(1, chips, hand_on, 0)
    lax.fori_loop(1, chips, finish, 0)
    to_near(0).wait()

    train_copy.wait()
    cut = rows.shape[2]
    gathered = rows[...].reshape(n * 16, cut)
    ends = 2 * cut
    tail = train_v.shape[1] - ends
    over = cut - tail

    def score(row_cols, train_cols):
        return dot_t(gathered[:, row_cols], train_v[:, train_cols], ((1,), (1,)))

    low = score(slice(0, cut), slice(0, cut))
    high = score(slice(0, cut), slice(cut, ends))
    tail_a = score(slice(0, tail), slice(ends, ends + tail))
    tail_b_low = score(slice(tail, cut), slice(ends, ends + over))
    tail_b_high = score(slice(0, tail - over), slice(ends + over, ends + tail))
    tail_c = score(slice(tail - over, cut), slice(ends, ends + tail))
    for d in range(n):
        at = 16 * (d % 2 * chips + d // 2)
        last = []
        for r in (6, 7):
            lo, hi = slice(at + r, at + r + 1), slice(at + 8 + r, at + 9 + r)
            last += [tail_a[lo, :], tail_b_low[lo, :] + tail_b_high[hi, :], tail_c[hi, :]]
        out[d * n_query : (d + 1) * n_query, :] = (
            low[at : at + n_query, :]
            + high[at + 8 : at + 8 + n_query, :]
            + jnp.concatenate(last, axis=0)
        )


def body(n, activations, out_grads, proj_in, proj_out, lengths, token_mask, query_ids, train_grads):
    tokens, n_in = activations.shape
    n_out = out_grads.shape[1]
    rank = proj_in.shape[1]
    n_query = query_ids.shape[0]
    owners = 2
    span_rows = rank // owners
    n_loads = 2 * (n_in // CHUNK + n_out // CHUNK) + 1
    smem = pl.BlockSpec(memory_space=pltpu.SMEM)
    vmem = pl.BlockSpec(memory_space=pltpu.VMEM)
    hbm = pl.BlockSpec(memory_space=pl.ANY)
    dma = pltpu.SemaphoreType.DMA
    flops = 2 * tokens * rank * (n_in + n_out) + 2 * train_grads.size * n * n_query
    return pl.pallas_call(
        functools.partial(kernel, n),
        out_shape=jax.ShapeDtypeStruct((n * n_query, train_grads.shape[0]), jnp.float32),
        in_specs=[smem, smem, vmem, hbm, hbm, hbm, hbm, hbm],
        out_specs=vmem,
        scratch_shapes=[
            pltpu.VMEM(activations.shape, jnp.bfloat16),
            pltpu.VMEM(out_grads.shape, jnp.bfloat16),
            pltpu.VMEM((rank, n_in), jnp.bfloat16),
            pltpu.VMEM((rank, n_out), jnp.bfloat16),
            pltpu.VMEM(train_grads.shape, jnp.bfloat16),
            pltpu.VMEM((owners, span_rows, 2 * rank), jnp.float32),
            pltpu.VMEM((owners, span_rows, 2 * rank), jnp.float32),
            pltpu.VMEM((max(n // owners, 1), span_rows, 2 * rank), jnp.float32),
            pltpu.VMEM((owners, span_rows, 2 * rank), jnp.float32),
            pltpu.VMEM((rank * 8, 2 * rank), jnp.float32),
            pltpu.VMEM((n, 16, rank * rank * n_query // 16), jnp.bfloat16),
            dma((n_loads,)),
            dma((owners,)),
            dma((owners,)),
            dma((max(n // owners, 1),)),
            dma((max(n // owners, 1),)),
            dma((owners,)),
            dma((owners,)),
            dma((n,)),
            dma((n,)),
        ],
        compiler_params=pltpu.CompilerParams(
            collective_id=0, has_side_effects=True, vmem_limit_bytes=56 * 1024 * 1024
        ),
        cost_estimate=pl.CostEstimate(flops=flops, bytes_accessed=16_000_000, transcendentals=0),
    )(
        lengths, query_ids, token_mask.reshape(1, tokens),
        activations, out_grads, proj_in.T, proj_out.T, train_grads,
    ).T


def solution(mesh):
    in_specs = (
        P(("groups", "dp"), None),
        P(("groups", "dp"), None),
        P(),
        P(),
        P(("groups", "dp")),
        P(("groups", "dp")),
        P(("groups", "dp")),
        P(("groups", "dp"), None),
    )
    out_specs = P(("groups", "dp"), None)
    run = functools.partial(body, mesh.shape["dp"])
    return jax.shard_map(run, mesh=mesh, in_specs=in_specs, out_specs=out_specs, check_vma=False)
```

```python
import functools

import jax
import jax.numpy as jnp
from jax import lax
from jax.experimental import pallas as pl
from jax.experimental.pallas import tpu as pltpu
from jax.sharding import PartitionSpec as P

MESH = pl.DeviceIdType.MESH
HIGHEST = lax.Precision.HIGHEST
CHUNK = 2048
PANEL = 4


def dot_t(a, b, dims, **kw):
    return lax.dot_general(a, b, (dims, ((), ())), preferred_element_type=jnp.float32, **kw)


def invert_pair(matrix):
    rank, width = matrix.shape
    tiles = [matrix[8 * t : 8 * t + 8, :] for t in range(rank // 8)]
    lane = lax.broadcasted_iota(jnp.int32, (8, width), 1)
    sub = lax.broadcasted_iota(jnp.int32, (8, width), 0)
    first = lane < rank
    column = jnp.where(first, lane, lane - rank)
    for base in range(0, rank, PANEL):
        own, start = base // 8, base % 8
        spread = [
            [
                jnp.where(
                    first,
                    jnp.broadcast_to(tile[:, base + j : base + j + 1], (8, width)),
                    jnp.broadcast_to(tile[:, rank + base + j : rank + base + j + 1], (8, width)),
                )
                for tile in tiles
            ]
            for j in range(PANEL)
        ]
        for j in range(PANEL):
            at = start + j
            here = sub == at
            at_col = column == base + j
            inv = 1.0 / spread[j][own][at : at + 1, :]
            row = jnp.where(at_col[0:1, :], 1.0, tiles[own][at : at + 1, :]) * inv
            for t in range(len(tiles)):
                new = jnp.where(at_col, 0.0, tiles[t]) - spread[j][t] * row
                tiles[t] = jnp.where(here, row, new) if t == own else new
            for k in range(j + 1, PANEL):
                factor = spread[k][own][at : at + 1, :] * inv
                for t in range(len(tiles)):
                    new = spread[k][t] - spread[j][t] * factor
                    spread[k][t] = jnp.where(here, factor, new) if t == own else new
    return jnp.concatenate(tiles, axis=0)


def kernel(
    n, lengths, query_ids, mask, act_hbm, grad_hbm, pin_hbm, pout_hbm, train_hbm, out,
    act_v, grad_v, pin_v, pout_v, train_v, part, landed, sums, total, wide, rows,
    load_sem, rs_send, rs_recv, ex_send, ex_recv, ag_send, ag_recv, row_send, row_recv,
):
    me = lax.axis_index("dp")
    tokens, n_in = act_hbm.shape
    n_out = grad_hbm.shape[1]
    rank = pin_hbm.shape[0]
    width = 2 * rank
    owners = part.shape[0]
    span_rows = part.shape[1]
    rep = n // owners

    barrier = pltpu.get_barrier_semaphore()

    chips = n // 2
    core = lax.rem(me, 2)
    near = me + 1 - 2 * core

    def greet(to):
        pl.semaphore_signal(barrier, inc=1, device_id={"dp": to}, device_id_type=MESH)

    def greet_chip(k, _):
        greet(lax.rem(me + 2 * k, n))
        return 0

    greet(near)
    lax.fori_loop(1, chips, greet_chip, 0)

    sem_at = 0
    plan = []
    for x_hbm, w_hbm, x_v, w_v, depth in (
        (act_hbm, pin_hbm, act_v, pin_v, n_in),
        (grad_hbm, pout_hbm, grad_v, pout_v, n_out),
    ):
        for c in range(depth // CHUNK):
            cols = slice(c * CHUNK, (c + 1) * CHUNK)
            copies = (
                pltpu.make_async_copy(w_hbm.at[:, cols], w_v.at[:, cols], load_sem.at[sem_at]),
                pltpu.make_async_copy(x_hbm.at[:, cols], x_v.at[:, cols], load_sem.at[sem_at + 1]),
            )
            sem_at += 2
            for copy in copies:
                copy.start()
            plan.append((copies, x_v, w_v, cols))
    train_copy = pltpu.make_async_copy(train_hbm, train_v, load_sem.at[sem_at])
    train_copy.start()

    accs = {}
    for copies, x_v, w_v, cols in plan:
        for copy in copies:
            copy.wait()
        upright = w_v[:, cols].astype(jnp.float32).T.astype(jnp.bfloat16)
        term = jnp.dot(x_v[:, cols], upright, preferred_element_type=jnp.float32)
        accs[id(x_v)] = accs[id(x_v)] + term if id(x_v) in accs else term
    act_proj, grad_proj = accs[id(act_v)], accs[id(grad_v)]

    slot = lax.broadcasted_iota(jnp.int32, (1, tokens), 1)
    n_resp = lengths.shape[0]
    span = tokens // n_resp
    response = slot // span
    length = jnp.zeros((1, tokens), jnp.int32)
    for r in range(n_resp):
        length = jnp.where(response == r, lengths[r], length)
    weight = jnp.where((slot - response * span < length) & (mask[...] == 1), 1.0, 0.0)

    both = jnp.concatenate([act_proj, grad_proj], axis=1)
    both_t = both.T * weight
    fisher = jnp.dot(both_t, both, precision=HIGHEST, preferred_element_type=jnp.float32)
    lane = lax.broadcasted_iota(jnp.int32, (rank, width), 1)
    packed = jnp.where(lane < rank, fisher[:rank, :], fisher[rank:, :])
    for c in range(owners):
        part[c] = packed[c * span_rows : (c + 1) * span_rows, :]

    pl.semaphore_wait(barrier, chips)

    team = me // owners
    seat = me - team * owners

    def peer(k):
        return lax.rem(seat + k, owners)

    def rs_copy(k):
        to = peer(k)
        return pltpu.make_async_remote_copy(
            src_ref=part.at[to], dst_ref=landed.at[k],
            send_sem=rs_send.at[k], recv_sem=rs_recv.at[k],
            device_id={"dp": team * owners + to}, device_id_type=MESH,
        )

    def start_rs(k, _):
        rs_copy(k).start()
        return 0

    lax.fori_loop(1, owners, start_rs, 0)

    n_query = query_ids.shape[0]
    grad_t = both_t[rank:, :]
    picked = jnp.concatenate(
        [jnp.where(response == query_ids[q], grad_t, 0.0) for q in range(n_query)], axis=0
    )
    chosen = jnp.dot(picked, act_proj, precision=HIGHEST, preferred_element_type=jnp.float32)

    def wait_rs(k, acc):
        rs_copy(k).wait()
        return acc + landed[k]

    mine = lax.fori_loop(1, owners, wait_rs, part[seat])
    if rep > 1:
        sums[0] = mine

        def ex_copy(k):
            return pltpu.make_async_remote_copy(
                src_ref=sums.at[0], dst_ref=sums.at[k],
                send_sem=ex_send.at[k], recv_sem=ex_recv.at[k],
                device_id={"dp": lax.rem(me + k * owners, n)}, device_id_type=MESH,
            )

        def start_ex(k, _):
            ex_copy(k).start()
            return 0

        def wait_ex(k, acc):
            ex_copy(k).wait()
            return acc + sums[k]

        lax.fori_loop(1, rep, start_ex, 0)
        mine = lax.fori_loop(1, rep, wait_ex, mine)
    total[seat] = mine

    def ag_copy(k):
        return pltpu.make_async_remote_copy(
            src_ref=total.at[seat], dst_ref=total.at[seat],
            send_sem=ag_send.at[k], recv_sem=ag_recv.at[k],
            device_id={"dp": team * owners + peer(k)}, device_id_type=MESH,
        )

    def start_ag(k, _):
        ag_copy(k).start()
        return 0

    def wait_ag(k, _):
        ag_copy(k).wait()
        return 0

    lax.fori_loop(1, owners, start_ag, 0)
    lax.fori_loop(1, owners, wait_ag, 0)

    summed = jnp.concatenate([total[c] for c in range(owners)], axis=0)
    row_at = lax.broadcasted_iota(jnp.int32, (rank, width), 0)
    left = lane < rank
    diag = row_at == jnp.where(left, lane, lane - rank)
    on_diag = jnp.where(diag, summed, 0.0)
    trace_act = jnp.sum(jnp.where(left, on_diag, 0.0), axis=(0, 1), keepdims=True)
    trace_grad = jnp.sum(jnp.where(left, 0.0, on_diag), axis=(0, 1), keepdims=True)
    scale = jnp.where(left, trace_act, trace_grad) / rank + 1e-06
    inverse = invert_pair(summed / scale + jnp.where(diag, 0.1, 0.0))

    swapped = pltpu.roll(inverse, rank, 1)
    inv_act_twice = jnp.where(left, inverse, swapped)
    inv_grad = swapped[:, :rank]
    right_done = jnp.dot(chosen, inv_act_twice, precision=HIGHEST, preferred_element_type=jnp.float32)
    for q in range(8):
        if q < n_query:
            value = jnp.dot(
                inv_grad, right_done[q * rank : (q + 1) * rank, :],
                precision=HIGHEST, preferred_element_type=jnp.float32,
            )
        else:
            value = jnp.zeros((rank, width), jnp.float32)
        wide[pl.ds(q, rank, stride=8), :] = value
    left8 = left[:8, :]
    pieces = [
        jnp.where(left8, wide[16 * p : 16 * p + 8, :], wide[16 * p + 8 : 16 * p + 16, :])
        for p in range(rank // 2)
    ]
    squares = pieces[0] * pieces[0]
    for piece in pieces[1:]:
        squares = squares + piece * piece
    mean = jnp.sum(squares, axis=1, keepdims=True) / (rank * rank)
    root = jnp.sqrt(mean + 1e-06)
    pieces = [piece / root for piece in pieces]
    sub8 = row_at[:8, :]
    body_count = rank // 2 * n_query // 8
    tail_count = rank // 2 - body_count
    third = n_query // 2
    packed_rows = []
    for p in range(body_count):
        tail, q = pieces[body_count + p % tail_count], p // tail_count
        last = jnp.where(sub8 == 6, tail[q : q + 1, :], tail[third + q : third + q + 1, :])
        packed_rows.append(jnp.where(sub8 < 6, pieces[p], last))
    half = body_count // 2
    mine_at = core * chips + me // 2
    for p in range(half):
        tile = jnp.concatenate([packed_rows[p], packed_rows[p + half]], axis=0)
        rows[mine_at, :, width * p : width * (p + 1)] = tile.astype(jnp.bfloat16)

    def send(block, to, k):
        return pltpu.make_async_remote_copy(
            src_ref=rows.at[block], dst_ref=rows.at[block],
            send_sem=row_send.at[k], recv_sem=row_recv.at[k],
            device_id={"dp": to}, device_id_type=MESH,
        )

    def to_chip(k):
        return send(mine_at, lax.rem(me + 2 * k, n), k)

    def to_near(k):
        return send(core * chips + lax.rem(me // 2 + chips - k, chips), near, chips + k)

    def start_chip(k, _):
        to_chip(k).start()
        return 0

    def hand_on(k, _):
        to_chip(k).wait_recv()
        to_near(k).start()
        return 0

    def finish(k, _):
        to_near(k).wait()
        to_chip(k).wait_send()
        return 0

    lax.fori_loop(1, chips, start_chip, 0)
    to_near(0).start()
    lax.fori_loop(1, chips, hand_on, 0)
    lax.fori_loop(1, chips, finish, 0)
    to_near(0).wait()

    train_copy.wait()
    cut = rows.shape[2]
    gathered = rows[...].reshape(n * 16, cut)
    ends = 2 * cut
    tail = train_v.shape[1] - ends
    over = cut - tail

    def score(row_cols, train_cols):
        return dot_t(gathered[:, row_cols], train_v[:, train_cols], ((1,), (1,)))

    low = score(slice(0, cut), slice(0, cut))
    high = score(slice(0, cut), slice(cut, ends))
    tail_a = score(slice(0, tail), slice(ends, ends + tail))
    tail_b_low = score(slice(tail, cut), slice(ends, ends + over))
    tail_b_high = score(slice(0, tail - over), slice(ends + over, ends + tail))
    tail_c = score(slice(tail - over, cut), slice(ends, ends + tail))
    for d in range(n):
        at = 16 * (d % 2 * chips + d // 2)
        last = []
        for r in (6, 7):
            lo, hi = slice(at + r, at + r + 1), slice(at + 8 + r, at + 9 + r)
            last += [tail_a[lo, :], tail_b_low[lo, :] + tail_b_high[hi, :], tail_c[hi, :]]
        out[d * n_query : (d + 1) * n_query, :] = (
            low[at : at + n_query, :]
            + high[at + 8 : at + 8 + n_query, :]
            + jnp.concatenate(last, axis=0)
        )


def body(n, activations, out_grads, proj_in, proj_out, lengths, token_mask, query_ids, train_grads):
    tokens, n_in = activations.shape
    n_out = out_grads.shape[1]
    rank = proj_in.shape[1]
    n_query = query_ids.shape[0]
    owners = 2
    span_rows = rank // owners
    n_loads = 2 * (n_in // CHUNK + n_out // CHUNK) + 1
    smem = pl.BlockSpec(memory_space=pltpu.SMEM)
    vmem = pl.BlockSpec(memory_space=pltpu.VMEM)
    hbm = pl.BlockSpec(memory_space=pl.ANY)
    dma = pltpu.SemaphoreType.DMA
    flops = 2 * tokens * rank * (n_in + n_out) + 2 * train_grads.size * n * n_query
    return pl.pallas_call(
        functools.partial(kernel, n),
        out_shape=jax.ShapeDtypeStruct((n * n_query, train_grads.shape[0]), jnp.float32),
        in_specs=[smem, smem, vmem, hbm, hbm, hbm, hbm, hbm],
        out_specs=vmem,
        scratch_shapes=[
            pltpu.VMEM(activations.shape, jnp.bfloat16),
            pltpu.VMEM(out_grads.shape, jnp.bfloat16),
            pltpu.VMEM((rank, n_in), jnp.bfloat16),
            pltpu.VMEM((rank, n_out), jnp.bfloat16),
            pltpu.VMEM(train_grads.shape, jnp.bfloat16),
            pltpu.VMEM((owners, span_rows, 2 * rank), jnp.float32),
            pltpu.VMEM((owners, span_rows, 2 * rank), jnp.float32),
            pltpu.VMEM((max(n // owners, 1), span_rows, 2 * rank), jnp.float32),
            pltpu.VMEM((owners, span_rows, 2 * rank), jnp.float32),
            pltpu.VMEM((rank * 8, 2 * rank), jnp.float32),
            pltpu.VMEM((n, 16, rank * rank * n_query // 16), jnp.bfloat16),
            dma((n_loads,)),
            dma((owners,)),
            dma((owners,)),
            dma((max(n // owners, 1),)),
            dma((max(n // owners, 1),)),
            dma((owners,)),
            dma((owners,)),
            dma((n,)),
            dma((n,)),
        ],
        compiler_params=pltpu.CompilerParams(
            collective_id=0, has_side_effects=True, vmem_limit_bytes=56 * 1024 * 1024
        ),
        cost_estimate=pl.CostEstimate(flops=flops, bytes_accessed=16_000_000, transcendentals=0),
    )(
        lengths, query_ids, token_mask.reshape(1, tokens),
        activations, out_grads, proj_in.T, proj_out.T, train_grads,
    ).T


def solution(mesh):
    in_specs = (
        P(("groups", "dp"), None),
        P(("groups", "dp"), None),
        P(),
        P(),
        P(("groups", "dp")),
        P(("groups", "dp")),
        P(("groups", "dp")),
        P(("groups", "dp"), None),
    )
    out_specs = P(("groups", "dp"), None)
    run = functools.partial(body, mesh.shape["dp"])
    return jax.shard_map(run, mesh=mesh, in_specs=in_specs, out_specs=out_specs, check_vma=False)
```
